32 devices in a mesh: band: 4 (over y, x), lon: 8 (over z, core).
Axes of the slice: x: 2, y: 2, z: 4, core: 2. Of those that a mesh axis runs over, the one named last changes fastest.
Arguments:
- members: bfloat16 [1536, 48, 256], P(('band', 'lon')), may hold values from -6 to 6
- obs_perts: bfloat16 [1536, 32, 256], P(('band', 'lon')), may hold values from -6 to 6
- innovations: bfloat16 [1536, 32], P(('band', 'lon')), may hold values from -12 to 12
- lists: int32 [256, 64], P(('band', 'lon')), may hold values from 0 to 1535, as said below
- placement: int32 [1536], replicated, may hold values from 0 to 1535, as said below
- obs_taper: float32 [256, 64, 32], P(('band', 'lon')), may hold values from 0.01 to 0.2
- state_taper: float32 [256, 64], P(('band', 'lon')), may hold values from 0.2 to 1
Outputs:
- analysis: bfloat16 [1536, 48, 256], P(('band', 'lon'))
The draws below stay inside these ranges and needn't reach their ends.
Inputs may be any that keep to these rules, and one draw needn't show every extreme that they name: `lists`: number the groups of 8 consecutive regions like the devices (band index times the lon count plus lon index) and call row // 48 a row's device. A group's entries name only blocks on the devices at band offset -1, 0 or 1 and lon offset -1, 0 or 1 (lon taken cyclically) from the group's own; from each such device that exists they name exactly 16 distinct blocks; every region names all 16 blocks of its own device; the 64 entries of one region are distinct. `placement`: A permutation of the block ids.
All inputs are finite; a program needn't handle non-finite values. Where the reference program divides by a largest or mean magnitude, that divisor is 1e-20 or more.
Results may differ from the reference program's by a relative error of at most 0.0055.
Values may be sent and summed in bfloat16 or wider, within the bound.
A program may use at most 128 MiB of HBM per device.

```python
import math
import jax
import jax.numpy as jnp
from jax import lax

K = 256
S = 48
P_SIZE = 32
NL = 64
R_DEV = 8
B_DEV = 48
NS_ITERS = 5
CAP = 16
NBLK = 1536
REGIONS = 256
N_BAND = 4
N_LON = 8


def shared_order(key):
    return jax.random.permutation(jax.random.fold_in(key, 101), NBLK).astype(jnp.int32)


def draw_placement(key, part):
    ordering = shared_order(key)
    return ordering


def draw_lists(key, part):
    ordering = shared_order(key)
    key = jax.random.fold_in(key, 11)
    inverse = jnp.argsort(ordering, stable=True).astype(jnp.int32)
    group_count = REGIONS // R_DEV
    others_total = 8 * CAP
    classes = jnp.arange(9, dtype=jnp.int32)
    other_class = jnp.concatenate([classes[:4], classes[5:]])
    slot_number = jnp.arange(others_total, dtype=jnp.int32)

    def inside_draw(sub_key):
        return jax.random.permutation(sub_key, B_DEV)[:CAP].astype(jnp.int32)

    def one_group(group_index):
        group_key = jax.random.fold_in(key, group_index)
        key_rows, key_fill, key_shuffle = jax.random.split(group_key, 3)
        band_home = group_index // N_LON
        lon_home = group_index % N_LON
        band_near = band_home + classes // 3 - 1
        lon_near = (lon_home + classes % 3 - 1) % N_LON
        present = (band_near >= 0) & (band_near < N_BAND)
        holder = jnp.clip(band_near, 0, N_BAND - 1) * N_LON + lon_near
        inside_rows = jax.vmap(inside_draw)(jax.random.split(key_rows, 9))
        block_rows = holder[:, None] * B_DEV + inside_rows
        own_rows = block_rows[4]
        other_rows = block_rows[other_class].reshape(-1)
        other_present = jnp.repeat(present[other_class], CAP)
        fill_keys = jax.random.split(key_fill, R_DEV)
        shuffle_keys = jax.random.split(key_shuffle, R_DEV)

        def one_region(region, fill_key, shuffle_key):
            shuffled = jax.random.permutation(fill_key, others_total).astype(jnp.int32)
            assigned = slot_number % R_DEV == region
            priority = jnp.where(other_present & assigned, shuffled, jnp.where(other_present, others_total + shuffled, 2 * others_total + shuffled))
            chosen = jnp.argsort(priority, stable=True)[:NL - CAP]
            picked = jnp.concatenate([own_rows, other_rows[chosen]])
            return picked[jax.random.permutation(shuffle_key, NL)]
        rows_out = jax.vmap(one_region)(jnp.arange(R_DEV, dtype=jnp.int32), fill_keys, shuffle_keys)
        return jnp.take(inverse, rows_out, axis=0)
    blocks = jax.vmap(one_group)(jnp.arange(group_count, dtype=jnp.int32))
    return blocks.reshape(REGIONS, NL).astype(jnp.int32)


def shard_levels(stream_key, extent, cuts, least, largest):
    gain, own = 1.0, jax.random.fold_in(stream_key, 6)
    for position, shards_of in cuts:
        heights = jnp.exp(jax.random.uniform(jax.random.fold_in(own, position), (shards_of,), jnp.float32, least / len(cuts), largest / len(cuts)))
        gain = gain * jnp.repeat(heights, extent[position] // shards_of).reshape([-1 if axis == position else 1 for axis in range(len(extent))])
    return gain


def scatter_about(key, extent, deviation, most, shards=(), kind=jnp.bfloat16):
    array = deviation * jax.random.normal(key, extent, jnp.float32)
    if shards:
        array = array * shard_levels(key, extent, shards, -0.22, 0.18)
    return jnp.clip(array, -most, most).astype(kind)


def setup_inputs(seed: int = 0) -> dict:
    keys = jax.random.split(jax.random.key(seed), 8)
    return {
        "members": scatter_about(keys[0], (NBLK, S, K), 1.0, 6.0, ((0, 32),)),
        "obs_perts": scatter_about(keys[1], (NBLK, P_SIZE, K), 1.0, 6.0, ((0, 32),)),
        "innovations": scatter_about(keys[2], (NBLK, P_SIZE), 3.0, 12.0, ((0, 32),)),
        "lists": draw_lists(jax.random.fold_in(keys[7], 71), 0),
        "placement": draw_placement(jax.random.fold_in(keys[7], 71), 0),
        "obs_taper": jnp.clip(jnp.exp(math.log(0.2) - 2.9957323 * jax.random.uniform(keys[5], (REGIONS, NL, P_SIZE), jnp.float32) ** shard_levels(keys[5], (REGIONS, NL, P_SIZE), ((0, 32),), -0.2, 0.2)), 0.01, 0.2),
        "state_taper": jnp.clip(jnp.exp(math.log(1.0) - 1.609438 * jax.random.uniform(keys[6], (REGIONS, NL), jnp.float32) ** shard_levels(keys[6], (REGIONS, NL), ((0, 32),), -0.2, 0.2)), 0.2, 1.0),
    }


def inverse_root(matrix, identity):
    current = matrix
    estimate = identity
    for iteration in range(NS_ITERS):
        factor = 1.5 * identity - 0.5 * jnp.dot(estimate, current, precision=lax.Precision.HIGHEST)
        current = jnp.dot(current, factor, precision=lax.Precision.HIGHEST)
        estimate = jnp.dot(factor, estimate, precision=lax.Precision.HIGHEST)
    return estimate

def region_mix(obs_blocks, innov_blocks, weights):
    identity = jnp.eye(K, dtype=jnp.float32)
    obs_float = obs_blocks.astype(jnp.float32)
    gram_matrix = jnp.einsum('jpk,jpl->kl', obs_float * weights[:, :, None], obs_float, precision=lax.Precision.HIGHEST)
    projection = jnp.einsum('jp,jpk->k', weights * innov_blocks.astype(jnp.float32), obs_float, precision=lax.Precision.HIGHEST)
    system = (K - 1.0) * identity + gram_matrix
    scale_top = jnp.max(lax.optimization_barrier(jnp.sum(jnp.abs(system), axis=1)))
    inverse_sqrt = inverse_root(system / scale_top, identity) / jnp.sqrt(scale_top)
    halfway = jnp.dot(inverse_sqrt, projection, precision=lax.Precision.HIGHEST)
    mean_weights = jnp.dot(inverse_sqrt, halfway, precision=lax.Precision.HIGHEST)
    mixing = jnp.sqrt(K - 1.0) * inverse_sqrt - identity + mean_weights[:, None]
    return mixing.astype(jnp.bfloat16)

def reference(members, obs_perts, innovations, lists, placement, obs_taper, state_taper):
    group_count = REGIONS // R_DEV
    entries = R_DEV * NL
    row_ids = jnp.take(placement, lists, axis=0).astype(jnp.int32).reshape(group_count, entries)
    weights_all = obs_taper.reshape(group_count, R_DEV, NL, P_SIZE)
    tapers_all = state_taper.reshape(group_count, R_DEV, NL)

    def one_region(packed_region):
        rows_here, weights, tapers = packed_region
        mixing = region_mix(obs_perts[rows_here], innovations[rows_here], weights)
        portion = jnp.einsum('jsk,kl->jsl', members[rows_here].astype(jnp.float32), mixing.astype(jnp.float32))
        return (portion * tapers[:, None, None]).astype(jnp.bfloat16)

    def one_group(summed, packed):
        group_rows, group_weights, group_tapers = packed
        region_rows = group_rows.reshape(R_DEV, NL)
        portions = lax.map(one_region, (region_rows, group_weights, group_tapers))
        portions = lax.optimization_barrier(portions).reshape(entries, S, K)
        matching = group_rows[:, None] == group_rows[None, :]
        first_match = jnp.argmax(matching, axis=1).astype(jnp.int32)
        shares = jnp.zeros((entries, S, K), jnp.float32).at[first_match].add(portions.astype(jnp.float32))
        shares = lax.optimization_barrier(shares.astype(jnp.bfloat16))
        summed = summed.at[group_rows].add(shares.astype(jnp.float32))
        return (summed, None)
    start = jnp.zeros(members.shape, jnp.float32)
    summed, unused = lax.scan(one_group, start, (row_ids, weights_all, tapers_all))
    return (members.astype(jnp.float32) + summed).astype(jnp.bfloat16)
```

```python
import functools

import jax
import jax.numpy as jnp
from jax import lax
from jax.experimental import pallas as pl
from jax.experimental.pallas import tpu as pltpu
from jax.sharding import PartitionSpec as P

NS_ITERS = 5
CAP = 16
NEAR = 9
OWN = 4
MESH = pl.DeviceIdType.MESH
NT = (((1,), (1,)), ((), ()))


def peer_of(direction, band_count, lon_count):
    band = lax.axis_index("band") + direction // 3 - 1
    lon = lax.rem(lax.axis_index("lon") + lax.rem(direction, 3) - 1 + lon_count, lon_count)
    exists = (band >= 0) & (band < band_count)
    return exists, (band, lon)


def greet(band_count, lon_count):
    barrier = pltpu.get_barrier_semaphore()
    for direction in range(NEAR):
        if direction != OWN:
            exists, device = peer_of(direction, band_count, lon_count)

            @pl.when(exists)
            def _():
                pl.semaphore_signal(barrier, inc=1, device_id=device, device_id_type=MESH)

    band = lax.axis_index("band")
    beside = (band > 0).astype(jnp.int32) + (band < band_count - 1).astype(jnp.int32)
    pl.semaphore_wait(barrier, 2 + 3 * beside)


def copy_to(direction, source, landing, send_sem, recv_sem, device):
    return pltpu.make_async_remote_copy(
        src_ref=source.at[direction],
        dst_ref=landing.at[8 - direction],
        send_sem=send_sem.at[direction],
        recv_sem=recv_sem.at[8 - direction],
        device_id=device,
        device_id_type=MESH,
    )


def copy_from(direction, source, landing, send_sem, recv_sem, device):
    return pltpu.make_async_remote_copy(
        src_ref=source.at[direction],
        dst_ref=landing.at[direction],
        send_sem=send_sem.at[direction],
        recv_sem=recv_sem.at[direction],
        device_id=device,
        device_id_type=MESH,
    )


def ask_kernel(band_count, lon_count, ask_ref, got_ref, send_sem, recv_sem):
    peer = functools.partial(peer_of, band_count=band_count, lon_count=lon_count)
    greet(band_count, lon_count)
    for direction in range(NEAR):
        if direction == OWN:
            continue
        exists, device = peer(direction)

        @pl.when(exists)
        def _():
            copy_to(direction, ask_ref, got_ref, send_sem, recv_sem, device).start()

        @pl.when(jnp.logical_not(exists))
        def _():
            got_ref[direction] = jnp.full(got_ref.shape[1:], -1.0, jnp.float32)

    got_ref[OWN] = ask_ref[OWN]
    for direction in range(NEAR):
        if direction == OWN:
            continue
        exists, device = peer(direction)

        @pl.when(exists)
        def _():
            copy_from(direction, ask_ref, got_ref, send_sem, recv_sem, device).wait()


def analysis_kernel(
    band_count,
    lon_count,
    ids_ref,
    back_ref,
    hit_ref,
    taper_ref,
    members_ref,
    obs_ref,
    weight_ref,
    push_ref,
    out_ref,
    obs_out,
    obs_in,
    state_out,
    state_in,
    share_out,
    share_in,
    gram,
    turned,
    proj,
    mix,
    scaled,
    obs_send,
    obs_recv,
    state_send,
    state_recv,
    share_send,
    share_recv,
):
    peer = functools.partial(peer_of, band_count=band_count, lon_count=lon_count)
    blocks, state_rows, ensemble = members_ref.shape
    obs_rows = obs_ref.shape[1]
    regions = weight_ref.shape[1]

    def edge(i):
        return lax.rem(2 * i + 3, 8)

    def corner(i):
        return 2 * i + 2 * (i // 2)

    def each(order, body):
        def step(i, carry):
            direction = order(i)
            exists, device = peer(direction)

            @pl.when(exists)
            def _():
                body(direction, device)

            return carry

        lax.fori_loop(0, 4, step, 0)

    def pack_obs(direction, target):
        def one(i, carry):
            at = pl.multiple_of(i * obs_rows, obs_rows)
            target[direction, pl.ds(at, obs_rows), :] = obs_ref[ids_ref[direction, i]]
            return carry

        lax.fori_loop(0, CAP, one, 0)

    def pack_state(direction, target):
        def one(i, carry):
            target[direction, i] = members_ref[ids_ref[direction, i]]
            return carry

        lax.fori_loop(0, CAP, one, 0)

    greet(band_count, lon_count)

    def send_obs(direction, device):
        pack_obs(direction, obs_out)
        copy_to(direction, obs_out, obs_in, obs_send, obs_recv, device).start()

    each(corner, send_obs)
    each(edge, send_obs)
    pack_obs(OWN, obs_in)

    def clear(r, carry):
        gram[r] = jnp.zeros((ensemble, ensemble), jnp.float32)
        return carry

    lax.fori_loop(0, regions, clear, 0)
    proj[...] = jnp.zeros_like(proj)

    def add_gram(direction):
        turned[...] = obs_in[direction].astype(jnp.float32).T
        proj[...] += jnp.dot(
            push_ref[direction], obs_in[direction], preferred_element_type=jnp.float32
        )

        def one(r, carry):
            left = (turned[...] * weight_ref[direction, pl.ds(r, 1), :]).astype(jnp.bfloat16)
            gram[r] += jnp.dot(left, obs_in[direction], preferred_element_type=jnp.float32)
            return carry

        lax.fori_loop(0, regions, one, 0)

    def take_obs(direction, device):
        copy_from(direction, obs_out, obs_in, obs_send, obs_recv, device).wait()
        add_gram(direction)

    def fill_state(direction, device):
        pack_state(direction, state_out)

    def send_state(direction, device):
        copy_to(direction, state_out, state_in, state_send, state_recv, device).start()

    add_gram(OWN)
    each(corner, fill_state)
    each(edge, fill_state)
    pack_state(OWN, state_in)
    each(edge, take_obs)
    each(corner, send_state)
    each(edge, send_state)
    each(corner, take_obs)

    rows = lax.broadcasted_iota(jnp.int32, (ensemble, ensemble), 0)
    columns = lax.broadcasted_iota(jnp.int32, (ensemble, ensemble), 1)
    identity = (rows == columns).astype(jnp.float32)

    def dot(a, b):
        return jnp.dot(
            a.astype(jnp.bfloat16), b.astype(jnp.bfloat16), preferred_element_type=jnp.float32
        )

    def total(a):
        return jnp.sum(jnp.sum(a, axis=1, keepdims=True), axis=0, keepdims=True)

    def transform(r0, width):
        span = range(width)
        scale, lead, rest, gain, part = [], [], [], [], []
        for k in span:
            system = (ensemble - 1.0) * identity + gram[r0 + k]
            sums = jnp.sum(jnp.abs(system), axis=1, keepdims=True)
            top = jnp.max(sums, axis=0, keepdims=True)
            inside = identity - system / top
            middle = total(inside * identity) * (1.0 / ensemble)
            scale.append(top)
            lead.append(middle)
            rest.append(inside - middle * identity)
            gain.append(1.0 + 0.5 * middle)
            part.append(0.5 * rest[k])
        for _ in range(NS_ITERS - 1):
            square = [dot(rest[k], rest[k]) for k in span]
            square = [2.0 * lead[k] * rest[k] + square[k] for k in span]
            cube = [dot(square[k], rest[k]) for k in span]
            for k in span:
                c = lead[k]
                slope = 0.75 + 0.25 * c
                rest[k] = (0.25 * c * c) * rest[k] + slope * square[k] + 0.25 * cube[k]
                lead[k] = c * c * slope
            cross = [dot(part[k], rest[k]) for k in span]
            for k in span:
                grow = 1.0 + 0.5 * lead[k]
                part[k] = (0.5 * gain[k]) * rest[k] + grow * part[k] + 0.5 * cross[k]
                gain[k] = gain[k] * grow
        for k in span:
            over = lax.rsqrt(scale[k])
            push = proj[pl.ds(r0 + k, 1), :] + proj[pl.ds(regions + r0 + k, 1), :]
            push = jnp.broadcast_to(push, (8, ensemble))
            halfway = (gain[k] * push + dot(push, part[k])) * over
            mean = (gain[k] * halfway + dot(halfway, part[k])) * over
            root = (gain[k] * identity + part[k]) * over
            across = (ensemble - 1.0) ** 0.5 * root - identity + mean[0:1]
            at = pl.multiple_of((r0 + k) * ensemble, ensemble)
            mix[pl.ds(at, ensemble), :] = across.T.astype(jnp.bfloat16)

    def quad(i, carry):
        transform(4 * i, 4)
        return carry

    lax.fori_loop(0, regions // 4, quad, 0)

    def increments(direction, target):
        def one(i, carry):
            block = state_in[direction, i].astype(jnp.float32)
            at = pl.multiple_of(i * state_rows, state_rows)
            for r in range(regions):
                scaled[pl.ds(at, state_rows), r * ensemble : (r + 1) * ensemble] = (
                    block * taper_ref[r, direction * CAP + i]
                ).astype(jnp.bfloat16)
            return carry

        lax.fori_loop(0, CAP, one, 0)
        made = jnp.dot(scaled[...], mix[...], preferred_element_type=jnp.float32)
        target[direction] = made.astype(jnp.bfloat16).reshape(CAP, state_rows, ensemble)

    def send_share(direction, device):
        copy_from(direction, state_out, state_in, state_send, state_recv, device).wait()
        increments(direction, share_out)
        copy_to(direction, share_out, share_in, share_send, share_recv, device).start()

    each(corner, send_share)
    each(edge, send_share)
    increments(OWN, share_in)

    def take_share(direction, device):
        copy_from(direction, share_out, share_in, share_send, share_recv, device).wait()

    each(edge, take_share)
    each(corner, take_share)
    for direction in range(NEAR):
        if direction // 3 != 1:
            exists, _ = peer(direction)

            @pl.when(jnp.logical_not(exists))
            def _():
                share_in[direction] = jnp.zeros(share_in.shape[1:], share_in.dtype)

    def combine(b, carry):
        result = members_ref[b].astype(jnp.float32)
        for direction in range(NEAR):
            share = share_in[direction, back_ref[direction, b]].astype(jnp.float32)
            result = result + share * hit_ref[direction, b]
        out_ref[b] = result.astype(jnp.bfloat16)
        return carry

    lax.fori_loop(0, blocks, combine, 0)


def local(band_count, lon_count, members, obs_perts, innovations, lists, placement, obs_taper, state_taper):
    block_count, state_rows, ensemble = members.shape
    obs_rows = obs_perts.shape[1]
    regions, list_len = lists.shape
    entries = regions * list_len
    pool = NEAR * CAP
    band_here = lax.axis_index("band")
    lon_here = lax.axis_index("lon")
    row_ids = jnp.take(placement, lists.reshape(-1), axis=0)
    holder = row_ids // block_count
    band_step = holder // lon_count - band_here
    lon_step = (holder % lon_count - lon_here + 1) % lon_count - 1
    neighbour = (band_step + 1) * 3 + lon_step + 1
    place = neighbour * block_count + row_ids % block_count
    named = place[:, None] == jnp.arange(NEAR * block_count, dtype=jnp.int32)[None, :]
    used = jnp.any(named, axis=0).reshape(NEAR, block_count)
    used_float = used.astype(jnp.float32)
    before = jnp.triu(jnp.ones((block_count, block_count), jnp.float32), 1)
    order = jnp.dot(used_float, before).astype(jnp.int32)
    caps = jnp.arange(CAP, dtype=jnp.int32)
    chosen = ((order[:, None, :] == caps[None, :, None]) & used[:, None, :]).astype(jnp.float32)
    block_ids = jnp.arange(block_count, dtype=jnp.float32)
    request = jnp.sum(chosen * block_ids, axis=2)
    slot_id = (order + CAP * jnp.arange(NEAR, dtype=jnp.int32)[:, None]).reshape(-1)
    slot = jnp.max(jnp.where(named, slot_id[None, :], 0), axis=1)
    slot_hot = (slot[:, None] == jnp.arange(pool, dtype=jnp.int32)[None, :]).astype(jnp.float32)
    slot_hot = slot_hot.reshape(regions, list_len, pool)

    lanes = 128
    innov = jnp.pad(innovations.astype(jnp.float32), ((0, 0), (0, lanes - obs_rows)))
    asked = jnp.pad(request[:, None, :], ((0, 0), (0, 7), (0, lanes - CAP)))
    message = jnp.concatenate(
        [jnp.broadcast_to(innov[None], (NEAR, block_count, lanes)), asked], axis=1
    )
    vmem = pl.BlockSpec(memory_space=pltpu.VMEM)
    smem = pl.BlockSpec(memory_space=pltpu.SMEM)
    got = pl.pallas_call(
        functools.partial(ask_kernel, band_count, lon_count),
        out_shape=jax.ShapeDtypeStruct(message.shape, jnp.float32),
        in_specs=[vmem],
        out_specs=vmem,
        scratch_shapes=[pltpu.SemaphoreType.DMA((NEAR,)), pltpu.SemaphoreType.DMA((NEAR,))],
        compiler_params=pltpu.CompilerParams(
            collective_id=0, has_side_effects=True, vmem_limit_bytes=16 * 2**20
        ),
    )(message)
    given = got[:, block_count, :CAP].astype(jnp.int32)
    ids = jnp.clip(given, 0, block_count - 1)
    match = given[:, None, :] == jnp.arange(block_count, dtype=jnp.int32)[None, :, None]
    back = jnp.max(jnp.where(match, caps[None, None, :], 0), axis=2)
    hit = jnp.any(match, axis=2).astype(jnp.float32)

    high = lax.Precision.HIGHEST
    weights = jnp.einsum("rjq,rjp->rqp", slot_hot, obs_taper, precision=high)
    tapers = jnp.sum(slot_hot * state_taper[:, :, None], axis=1)
    innov_pool = jnp.einsum("nib,nbp->nip", chosen, got[:, :block_count, :obs_rows])
    push = weights.reshape(regions, NEAR, CAP, obs_rows) * innov_pool[None]

    def by_neighbour(a):
        return a.reshape(regions, NEAR, CAP * obs_rows).transpose(1, 0, 2)

    weights = by_neighbour(weights)
    push = by_neighbour(push)
    push_high = push.astype(jnp.bfloat16)
    push_low = (push - push_high.astype(jnp.float32)).astype(jnp.bfloat16)
    push = jnp.concatenate([push_high, push_low], axis=1)

    obs_pool = pltpu.VMEM((NEAR, CAP * obs_rows, ensemble), jnp.bfloat16)
    state_pool = pltpu.VMEM((NEAR, CAP, state_rows, ensemble), jnp.bfloat16)
    sems = pltpu.SemaphoreType.DMA((NEAR,))
    return pl.pallas_call(
        functools.partial(analysis_kernel, band_count, lon_count),
        out_shape=jax.ShapeDtypeStruct(members.shape, members.dtype),
        in_specs=[smem, smem, smem, smem, vmem, vmem, vmem, vmem],
        out_specs=vmem,
        scratch_shapes=[
            obs_pool,
            obs_pool,
            state_pool,
            state_pool,
            state_pool,
            state_pool,
            pltpu.VMEM((regions, ensemble, ensemble), jnp.float32),
            pltpu.VMEM((ensemble, CAP * obs_rows), jnp.float32),
            pltpu.VMEM((2 * regions, ensemble), jnp.float32),
            pltpu.VMEM((regions * ensemble, ensemble), jnp.bfloat16),
            pltpu.VMEM((CAP * state_rows, regions * ensemble), jnp.bfloat16),
            sems,
            sems,
            sems,
            sems,
            sems,
            sems,
        ],
        compiler_params=pltpu.CompilerParams(
            collective_id=1, has_side_effects=True, vmem_limit_bytes=56 * 2**20
        ),
    )(ids, back, hit, tapers, members, obs_perts, weights, push)


def solution(mesh):
    in_specs = (
        P(("band", "lon"), None, None),
        P(("band", "lon"), None, None),
        P(("band", "lon"), None),
        P(("band", "lon"), None),
        P(),
        P(("band", "lon"), None, None),
        P(("band", "lon"), None),
    )
    out_specs = P(("band", "lon"), None, None)
    body = functools.partial(local, mesh.shape["band"], mesh.shape["lon"])
    return jax.shard_map(body, mesh=mesh, in_specs=in_specs, out_specs=out_specs, check_vma=False)
```
